256 devices in a mesh: row: 128 (over x_lo, y, z, core), col: 2 (over x_hi).
Axes of the slice: x: 4 (x_hi: 2, x_lo: 2; x = x_hi * 2 + x_lo), y: 4, z: 8, core: 2. Of those that a mesh axis runs over, the one named last changes fastest.
Arguments:
- row_embed: bfloat16 [300, 131072], P(None, 'row'), may hold values from -1.796875 to 1.796875
- col_embed: bfloat16 [300, 2, 2048], P(None, 'col', 'row'), may hold values from -1.796875 to 1.796875
- counts: int32 [131072, 2, 2048], P('row', 'col'), may hold values from 0 to 64, as said below
- occupancy: int32 [1024, 2, 16], P('row', 'col'), may hold values from 0 to 1, as said below
- row_marg: int32 [131072], P('row'), may hold values from 2000 to 199999
- col_marg: int32 [2, 2048], P('col', 'row'), may hold values from 2000 to 199999
- log_total: float32 [1], replicated, may hold values from 18 to 22
Outputs:
- grad_rows: float32 [300, 131072], P(None, 'row')
- grad_cols: float32 [300, 2, 2048], P(None, 'col', 'row')
The draws below stay inside these ranges and needn't reach their ends.
Inputs may be any that keep to these rules, and one draw needn't show every extreme that they name: counts of the band's cells; zero in part of the cells. `occupancy`: the share of tiles marked 1 differs from row tile to row tile.
All inputs are finite; a program needn't handle non-finite values.
Results may differ from the reference program's by a relative error of at most 0.0018.
Values may be sent and summed in bfloat16 or wider, within the bound.
No kernel may reach another device: no remote copies, remote signals or barrier semaphores. Data moves between devices by JAX's collectives and lax.ppermute only.
A program may use at most 64 MiB of HBM per device.

```python
import math
import jax
import jax.numpy as jnp
from jax import lax

D = 300
TILE = 128
ROW_DEV = 1024
ROWS = 131072
BAND = 2048
BANDS = 2
COLS = 4096
ROW_TILES = 1024
BAND_TILES = 16


def draw_counts(key, part):
    present = jax.random.randint(jax.random.fold_in(key, 11), (ROWS, BANDS, BAND), 0, 2)
    values = jax.random.randint(jax.random.fold_in(key, 12), (ROWS, BANDS, BAND), 1, 65)
    result = (present * values).astype(jnp.int32)
    return result.at[0, 0, 0].set(64)


def draw_occupancy(key, part):
    levels = jax.random.randint(jax.random.fold_in(key, 21), (ROW_TILES, 1, 1), 1, 9)
    rolls = jax.random.randint(jax.random.fold_in(key, 22), (ROW_TILES, BANDS, BAND_TILES), 0, 8)
    return (rolls < levels).astype(jnp.int32)


def with_ends(values, rng, smallest, high):
    longest = values.shape.index(max(values.shape))
    spots = []
    for shift in (0, 1):
        where = [jax.random.randint(jax.random.fold_in(rng, axis), (), 0, length) for axis, length in enumerate(values.shape)]
        where[longest] = (where[longest] + shift) % values.shape[longest]
        spots.append(tuple(where))
    return values.at[spots[0]].set(smallest).at[spots[1]].set(high)


def block_scale(own_key, extent, shards, smallest, high):
    gain = 1.0
    for axis_at, blocks in shards:
        draws = jax.random.uniform(jax.random.fold_in(jax.random.fold_in(own_key, 6), axis_at), (blocks,), jnp.float32, smallest / len(shards), high / len(shards))
        gain = gain * jnp.repeat(jnp.exp(draws), extent[axis_at] // blocks).reshape((-1,) + (1,) * (len(extent) - 1 - axis_at))
    return gain


def normal_values(stream_key, extent, spread, most, shards=(), held_as=jnp.bfloat16):
    values = spread * jax.random.normal(stream_key, extent, jnp.float32)
    if shards:
        values = values * block_scale(stream_key, extent, shards, -0.22, 0.18)
    return jnp.clip(values, -most, most).astype(held_as)


def setup_inputs(seed: int = 0) -> dict:
    seeds = jax.random.split(jax.random.key(seed), 8)
    return {
        "row_embed": normal_values(seeds[0], (D, ROWS), 0.3, 1.796875, ((1, 128),)),
        "col_embed": normal_values(seeds[1], (D, BANDS, BAND), 0.3, 1.796875, ((1, 2), (2, 128))),
        "counts": draw_counts(jax.random.fold_in(seeds[7], 71), 0),
        "occupancy": draw_occupancy(jax.random.fold_in(seeds[7], 71), 0),
        "row_marg": with_ends(jax.random.randint(seeds[4], (ROWS,), 2000, 200000), jax.random.fold_in(seeds[4], 1), 2000, 199999).astype(jnp.int32),
        "col_marg": with_ends(jax.random.randint(seeds[5], (BANDS, BAND), 2000, 200000), jax.random.fold_in(seeds[5], 1), 2000, 199999).astype(jnp.int32),
        "log_total": jnp.clip(jax.random.uniform(seeds[6], (1,), jnp.float32, 18.0, 22.0), 18.0, 22.0),
    }


def cell_slope(scores, count_part, log_row_part, log_col_all, log_base):
    count_values = count_part.astype(jnp.float32)
    log_ratio = jnp.log(jnp.maximum(count_values, 1.0)) + (log_base - log_row_part[:, None] - log_col_all[None, :])
    score_gap = scores - log_ratio
    return jnp.where(count_part > 0, (0.1 + 0.25 * jnp.sqrt(count_values)) * score_gap, jax.nn.sigmoid(score_gap))

def reference(row_embed, col_embed, counts, occupancy, row_marg, col_marg, log_total):
    col_matrix = col_embed.reshape(D, COLS)
    count_matrix = counts.reshape(ROWS, COLS)
    occ_matrix = occupancy.reshape(ROW_TILES, COLS // TILE).astype(jnp.float32)
    log_col_all = jnp.log(col_marg.reshape(COLS).astype(jnp.float32))
    log_row = jnp.log(row_marg.astype(jnp.float32))
    log_base = log_total[0]
    block_tiles = ROW_DEV // TILE

    def row_block(col_total, block_index):
        first_row = (block_index * ROW_DEV).astype(jnp.int32)
        row_part = lax.dynamic_slice_in_dim(row_embed, first_row, ROW_DEV, 1)
        count_part = lax.dynamic_slice_in_dim(count_matrix, first_row, ROW_DEV, 0)
        log_row_part = lax.dynamic_slice_in_dim(log_row, first_row, ROW_DEV, 0)
        occ_part = lax.dynamic_slice_in_dim(occ_matrix, (block_index * block_tiles).astype(jnp.int32), block_tiles, 0)
        scores = jnp.dot(row_part.T, col_matrix, preferred_element_type=jnp.float32)
        slopes = cell_slope(scores, count_part, log_row_part, log_col_all, log_base)
        masked = slopes.reshape(block_tiles, TILE, COLS // TILE, TILE) * occ_part[:, None, :, None]
        residual = masked.reshape(ROW_DEV, COLS).astype(jnp.bfloat16)
        row_grads = jnp.dot(col_matrix, residual.T, preferred_element_type=jnp.float32)
        col_total = col_total + jnp.dot(row_part, residual, preferred_element_type=jnp.float32)
        return (col_total, row_grads)
    col_total, row_grads = lax.scan(row_block, jnp.zeros((D, COLS), jnp.float32), jnp.arange(ROWS // ROW_DEV, dtype=jnp.int32))
    grad_rows = row_grads.transpose(1, 0, 2).reshape(D, ROWS) * (1.0 / math.sqrt(COLS))
    grad_cols = (col_total * (1.0 / math.sqrt(ROWS))).reshape(D, BANDS, BAND)
    return (grad_rows, grad_cols)
```

```python
import functools
import math

import jax
import jax.numpy as jnp
from jax import lax
from jax.experimental import pallas as pl
from jax.experimental.pallas import tpu as pltpu
from jax.sharding import Mesh, PartitionSpec as P

SPLIT = (2, 4, 8, 2, 2)
AXES = ("xl", "y", "z", "core", "xh")
ROW = ("xl", "y", "z", "core")
TILE = 128
WIDE = 384
BLOCK = 256
PACK = 40
VMEM_LIMIT = 32 * 1024 * 1024
HALF_LIMIT = 48 * 1024 * 1024
SWAP = [(0, 1), (1, 0)]


def three_parts(values):
    high = values.astype(jnp.bfloat16).astype(jnp.float32)
    rest = values - high
    middle = rest.astype(jnp.bfloat16).astype(jnp.float32)
    return high, middle, rest - middle


def prep_cols(embed_ref, marg_ref, out_ref):
    copies, words, wide = out_ref.shape
    depth = embed_ref.shape[1]
    log_col = jnp.log(marg_ref[...].astype(jnp.float32))
    square = (words, words)
    same = lax.broadcasted_iota(jnp.int32, square, 0) == lax.broadcasted_iota(jnp.int32, square, 1)
    spread = jnp.where(same, jnp.broadcast_to(log_col, square), 0.0).sum(axis=1, keepdims=True)
    high, middle, low = three_parts(spread)
    lane = lax.broadcasted_iota(jnp.int32, (words, wide - 256), 1) + 256
    tail = jnp.where(lane == depth, high, 0.0)
    tail = jnp.where(lane == depth + 1, middle, tail)
    tail = jnp.where(lane == depth + 2, low, tail)
    tail = jnp.where((lane >= depth + 3) & (lane < depth + 6), 1.0, tail)
    embed = embed_ref[...].astype(jnp.float32)
    padded = jnp.concatenate([embed, jnp.zeros((words, wide - depth), jnp.float32)], axis=1)
    block = jnp.concatenate([padded[:, :256], padded[:, 256:] + tail], axis=1).astype(jnp.bfloat16)
    for copy in range(copies):
        out_ref[copy] = block


def prep_rows(embed_ref, marg_ref, total_ref, wide_ref, turned_ref):
    depth, rows = embed_ref.shape
    wide = wide_ref.shape[0]
    log_row = jnp.log(marg_ref[...].astype(jnp.float32)) - total_ref[0]
    high, middle, low = three_parts(log_row)
    start = depth - depth % 8
    line = lax.broadcasted_iota(jnp.int32, (wide - start, rows), 0) + start
    tail = jnp.where((line >= depth) & (line < depth + 3), 1.0, 0.0)
    tail = jnp.where(line == depth + 3, high, tail)
    tail = jnp.where(line == depth + 4, middle, tail)
    tail = jnp.where(line == depth + 5, low, tail)
    embed = embed_ref[...].astype(jnp.float32)
    padded = jnp.concatenate([embed, jnp.zeros((wide - depth, rows), jnp.float32)], axis=0)
    whole = jnp.concatenate([padded[:start], padded[start:] + tail], axis=0)
    wide_ref[...] = whole.astype(jnp.bfloat16)
    turned_ref[...] = whole.T.astype(jnp.bfloat16)


def half_step(first, place, occ_ref, count_ref, wide_ref, turned_ref, own_ref, peer_ref, *rest):
    if first:
        row_out, keep_ref, send_ref, turned_cols, residual_ref, held, arrived = rest
    else:
        row_in, row_out, keep_ref, send_ref, turned_cols, residual_ref, held, arrived = rest
    which, core = place[0], place[1]
    chips, words, wide = own_ref.shape
    depth_rows = row_out.shape[0]
    rows, width = residual_ref.shape
    tiles = width // TILE
    blocks = rows // BLOCK

    def fetch(step):
        return pltpu.make_async_copy(
            count_ref.at[
                pl.ds(step * BLOCK, BLOCK), pl.ds(pl.multiple_of(which * tiles, tiles), tiles), :
            ],
            held.at[step],
            arrived.at[step],
        )

    for step in range(blocks):
        fetch(step).start()

    own, peer = own_ref[...], peer_ref[...]
    low = jnp.where(core == 0, own, peer)
    high = jnp.where(core == 0, peer, own)
    pair = jnp.concatenate([low[:, None], high[:, None]], axis=1)
    turned_cols[...] = pair.reshape(width, wide).T
    @pl.loop(0, blocks)
    def _(step):
        fetch(step).wait()
        count_flat = held.at[step].reshape(BLOCK * tiles, TILE)
        row_block = turned_ref[pl.ds(pl.multiple_of(step * BLOCK, BLOCK), BLOCK), :]
        for chunk in range(width // 256):
            cols = turned_cols[:, chunk * 256 : (chunk + 1) * 256]
            gap_base = jnp.dot(row_block, cols, preferred_element_type=jnp.float32)
            parts = []
            for side in range(2):
                tile = chunk * 2 + side
                cnt = count_flat[pl.ds(tile, BLOCK, stride=tiles), :]
                at_least = jnp.maximum(cnt.astype(jnp.float32), 1.0)
                gap = gap_base[:, side * TILE : (side + 1) * TILE] - jnp.log(at_least)
                slope = jnp.where(
                    cnt > 0,
                    (0.1 + 0.25 * (at_least * lax.rsqrt(at_least))) * gap,
                    1.0 / (1.0 + jnp.exp(-gap)),
                )
                pieces = []
                for sub in range(BLOCK // TILE):
                    mark = occ_ref[step * (BLOCK // TILE) + sub, which * tiles + tile]
                    pieces.append(slope[sub * TILE : (sub + 1) * TILE] * mark.astype(jnp.float32))
                parts.append(jnp.concatenate(pieces, axis=0).astype(jnp.bfloat16))
            residual_ref[
                pl.ds(pl.multiple_of(step * BLOCK, BLOCK), BLOCK), chunk * 256 : (chunk + 1) * 256
            ] = jnp.concatenate(parts, axis=1)

    row_total = lax.dot_general(
        turned_cols[:depth_rows, :], residual_ref[...], (((1,), (1,)), ((), ())),
        preferred_element_type=jnp.float32,
    )
    if not first:
        row_total = row_total + row_in[...]
    row_out[...] = row_total.astype(row_out.dtype)
    col_sum = jnp.dot(
        wide_ref[:depth_rows, :], residual_ref[...], preferred_element_type=jnp.float32
    )
    filled = jnp.concatenate([col_sum, jnp.zeros((wide - depth_rows, width), jnp.float32)], axis=0)
    words_first = filled.T.reshape(chips, 2, 2, 8, wide)
    lane = lax.broadcasted_iota(jnp.int32, (8, TILE), 1)
    for chip in range(chips):
        packed = []
        for side in range(2):
            block = words_first[chip, side]
            last = jnp.where(
                lane < 64, block[0, :, 256:], pltpu.roll(block[1, :, 256:], 64, 1)
            )
            packed.append(
                jnp.concatenate(
                    [block[0, :, :128], block[1, :, :128], block[0, :, 128:256],
                     block[1, :, 128:256], last], axis=0)
            )
        keep_ref[chip] = jnp.where(core == 0, packed[0], packed[1])
        send_ref[chip] = jnp.where(core == 0, packed[1], packed[0])


def run_half(first, place, occ, count_view, wide_rows, turned_rows, own, peer, row_in):
    rows = turned_rows.shape[0]
    chips, words, wide = own.shape
    width = chips * 2 * words
    depth_rows = 304
    smem = pl.BlockSpec(memory_space=pltpu.SMEM)
    vmem = pl.BlockSpec(memory_space=pltpu.VMEM)
    operands = [place, occ, count_view, wide_rows, turned_rows, own, peer]
    if not first:
        operands.append(row_in)
    chunk = jax.ShapeDtypeStruct((chips, PACK, TILE), jnp.float32)
    return pl.pallas_call(
        functools.partial(half_step, first),
        in_specs=[smem, smem, pl.BlockSpec(memory_space=pltpu.HBM)] + [vmem] * (len(operands) - 3),
        out_specs=[vmem] * 3,
        scratch_shapes=[
            pltpu.VMEM((wide, width), jnp.bfloat16),
            pltpu.VMEM((rows, width), jnp.bfloat16),
            pltpu.VMEM((rows // BLOCK, BLOCK, width // TILE, TILE), jnp.int32),
            pltpu.SemaphoreType.DMA((rows // BLOCK,)),
        ],
        out_shape=[
            jax.ShapeDtypeStruct((depth_rows, rows), jnp.float32 if first else jnp.bfloat16),
            chunk,
            chunk,
        ],
        compiler_params=pltpu.CompilerParams(vmem_limit_bytes=HALF_LIMIT),
        cost_estimate=pl.CostEstimate(
            flops=6 * rows * width * 300, bytes_accessed=8 * rows * width // 2,
            transcendentals=rows * width,
        ),
    )(*operands)


def join(place, keep_a, got_a, keep_b, got_b, out_ref):
    chips = keep_a.shape[0]
    which = place[0]
    for at, keep, got in ((which, keep_a, got_a), (1 - which, keep_b, got_b)):
        for chip in range(chips):
            out_ref[at * chips + chip] = (keep[chip] + got[chip]).astype(jnp.bfloat16)


def finish(row_scale, col_scale, mine_ref, theirs_ref, got_ref, rows_ref, cols_ref):
    depth = rows_ref.shape[0]
    both = mine_ref[...].astype(jnp.float32) + theirs_ref[...].astype(jnp.float32)
    rows_ref[...] = both[:depth] * row_scale
    total = got_ref[...].astype(jnp.float32).sum(axis=0) * col_scale
    last = total[32:40]
    turned = pltpu.roll(last, 64, 1)
    cols_ref[0:8, :] = jnp.concatenate([total[0:8], total[16:24], last], axis=1)[:, :depth]
    cols_ref[8:16, :] = jnp.concatenate([total[8:16], total[24:32], turned], axis=1)[:, :depth]


def body(row_embed, col_embed, counts, occupancy, row_marg, col_marg, log_total):


    depth, rows = row_embed.shape
    words = col_embed.shape[2]
    core = lax.axis_index("core")
    xl = lax.axis_index("xl")
    params = pltpu.CompilerParams(vmem_limit_bytes=VMEM_LIMIT)
    smem = pl.BlockSpec(memory_space=pltpu.SMEM)
    vmem = pl.BlockSpec(memory_space=pltpu.VMEM)

    fan_out = pl.pallas_call(
        prep_cols,
        out_shape=jax.ShapeDtypeStruct((32, words, WIDE), jnp.bfloat16),
        compiler_params=params,
    )(col_embed[:, 0, :].T, col_marg)
    quarter = lax.all_to_all(fan_out, ("y", "z"), 0, 0, tiled=True)
    wide_rows, turned_rows = pl.pallas_call(
        prep_rows,
        in_specs=[vmem, vmem, smem],
        out_shape=[
            jax.ShapeDtypeStruct((WIDE, rows), jnp.bfloat16),
            jax.ShapeDtypeStruct((rows, WIDE), jnp.bfloat16),
        ],
        compiler_params=params,
        cost_estimate=pl.CostEstimate(flops=rows * WIDE, bytes_accessed=4 * rows * WIDE, transcendentals=0),
    )(row_embed, row_marg[None, :], log_total)
    count_view = counts.reshape(rows, 16, TILE)
    occ = occupancy[:, 0, :]

    peer = lax.ppermute(quarter, "core", SWAP)
    far = lax.ppermute(quarter, "xl", SWAP)
    far_peer = lax.ppermute(far, "core", SWAP)
    row_part, keep_a, send_a = run_half(
        True, jnp.stack([xl, core]), occ, count_view, wide_rows, turned_rows, quarter, peer, None
    )
    got_a = lax.ppermute(send_a, "core", SWAP)
    mine, keep_b, send_b = run_half(
        False, jnp.stack([1 - xl, core]), occ, count_view, wide_rows, turned_rows, far, far_peer,
        row_part,
    )
    got_b = lax.ppermute(send_b, "core", SWAP)
    theirs = lax.ppermute(mine, "xh", SWAP)

    outgoing = pl.pallas_call(
        join,
        in_specs=[smem, vmem, vmem, vmem, vmem],
        out_shape=jax.ShapeDtypeStruct((64, PACK, TILE), jnp.bfloat16),
        compiler_params=params,
    )(xl[None], keep_a, got_a, keep_b, got_b)
    arrived = lax.all_to_all(outgoing, ("xl", "y", "z"), 0, 0, tiled=True)
    grad_rows, grad_cols = pl.pallas_call(
        functools.partial(finish, 1.0 / math.sqrt(words * 256), 1.0 / math.sqrt(rows * 128)),
        in_specs=[vmem, vmem, vmem],
        out_specs=[vmem, vmem],
        out_shape=[
            jax.ShapeDtypeStruct((depth, rows), jnp.float32),
            jax.ShapeDtypeStruct((words, depth), jnp.float32),
        ],
        compiler_params=params,
    )(mine, theirs, arrived)
    return (grad_rows, grad_cols.T[:, None, :])


def solution(mesh):
    fine = Mesh(mesh.devices.reshape(SPLIT), AXES)
    placed = (
        P(None, ROW),
        P(None, "xh", ROW),
        P(ROW, "xh", None),
        P(ROW, "xh", None),
        P(ROW),
        P("xh", ROW),
        P(),
    )
    return jax.shard_map(
        body,
        mesh=fine,
        in_specs=placed,
        out_specs=(P(None, ROW), P(None, "xh", ROW)),
        check_vma=False,
    )
```

```python
import functools
import math

import jax
import jax.numpy as jnp
from jax import lax
from jax.experimental import pallas as pl
from jax.experimental.pallas import tpu as pltpu
from jax.sharding import Mesh, PartitionSpec as P

SPLIT = (2, 4, 8, 2, 2)
AXES = ("xl", "y", "z", "core", "xh")
ROW = ("xl", "y", "z", "core")
TILE = 128
WIDE = 384
BLOCK = 256
PACK = 40
VMEM_LIMIT = 24 * 1024 * 1024
HALF_LIMIT = 48 * 1024 * 1024
SWAP = [(0, 1), (1, 0)]


def three_parts(values):
    high = values.astype(jnp.bfloat16).astype(jnp.float32)
    rest = values - high
    middle = rest.astype(jnp.bfloat16).astype(jnp.float32)
    return high, middle, rest - middle


def prep_cols(embed_ref, marg_ref, out_ref):
    copies = out_ref.shape[0]
    words, depth = embed_ref.shape
    log_col = jnp.log(marg_ref[...].astype(jnp.float32))
    square = (words, words)
    same = lax.broadcasted_iota(jnp.int32, square, 0) == lax.broadcasted_iota(jnp.int32, square, 1)
    spread = jnp.where(same, jnp.broadcast_to(log_col, square), 0.0).sum(axis=1, keepdims=True)
    high, middle, low = three_parts(spread)
    embed = embed_ref[...].astype(jnp.float32)
    lane = lax.broadcasted_iota(jnp.int32, (words, WIDE - 256), 1) + 256
    tail = jnp.where(lane == depth, high, 0.0)
    tail = jnp.where(lane == depth + 1, middle, tail)
    tail = jnp.where(lane == depth + 2, low, tail)
    tail = jnp.where((lane >= depth + 3) & (lane < depth + 6), 1.0, tail)
    padded = jnp.concatenate([embed, jnp.zeros((words, WIDE - depth), jnp.float32)], axis=1)
    tail = tail + padded[:, 256:]
    half_lane = lax.broadcasted_iota(jnp.int32, (8, TILE), 1)
    last = jnp.where(half_lane < 64, tail[:8], pltpu.roll(tail[8:], 64, 1))
    block = jnp.concatenate([padded[:, :128], padded[:, 128:256], last], axis=0).astype(jnp.bfloat16)
    for copy in range(copies):
        out_ref[copy] = block


def unpack_words(packed):
    blocks = packed.astype(jnp.float32)
    last = blocks[:, 32:40, :]
    lane = lax.broadcasted_iota(jnp.int32, last.shape, 2)
    front = jnp.where(lane < 64, last, 0.0)
    back = jnp.where(lane < 64, pltpu.roll(last, 64, 2), 0.0)
    tail = jnp.concatenate([front, back], axis=1)
    whole = jnp.concatenate([blocks[:, :16, :], blocks[:, 16:32, :], tail], axis=2)
    return whole.astype(jnp.bfloat16)


def prep_rows(embed_ref, marg_ref, total_ref, wide_ref, turned_ref):
    depth, rows = embed_ref.shape
    wide = wide_ref.shape[0]
    log_row = jnp.log(marg_ref[...].astype(jnp.float32)) - total_ref[0]
    high, middle, low = three_parts(log_row)
    start = depth - depth % 8
    line = lax.broadcasted_iota(jnp.int32, (wide - start, rows), 0) + start
    tail = jnp.where((line >= depth) & (line < depth + 3), 1.0, 0.0)
    tail = jnp.where(line == depth + 3, high, tail)
    tail = jnp.where(line == depth + 4, middle, tail)
    tail = jnp.where(line == depth + 5, low, tail)
    embed = embed_ref[...].astype(jnp.float32)
    padded = jnp.concatenate([embed, jnp.zeros((wide - depth, rows), jnp.float32)], axis=0)
    whole = jnp.concatenate([padded[:start], padded[start:] + tail], axis=0)
    wide_ref[...] = whole.astype(jnp.bfloat16)
    turned_ref[...] = whole.T.astype(jnp.bfloat16)


def half_step(first, occ_ref, count_ref, wide_ref, turned_ref, own_ref, peer_ref, *rest):
    if first:
        row_out, keep_ref, send_ref, turned_cols, residual_ref, held, arrived = rest
    else:
        row_in, row_out, keep_ref, send_ref, turned_cols, residual_ref, held, arrived = rest
    xl, core = lax.axis_index("xl"), lax.axis_index("core")
    which = xl if first else 1 - xl
    chips = own_ref.shape[0]
    wide = wide_ref.shape[0]
    depth_rows = 304
    rows, width = residual_ref.shape
    tiles = width // TILE
    blocks = rows // BLOCK

    def fetch(step):
        return pltpu.make_async_copy(
            count_ref.at[
                pl.ds(step * BLOCK, BLOCK), pl.ds(pl.multiple_of(which * tiles, tiles), tiles), :
            ],
            held.at[step],
            arrived.at[step],
        )

    for step in range(blocks):
        fetch(step).start()

    own, peer = unpack_words(own_ref[...]), unpack_words(peer_ref[...])
    low = jnp.where(core == 0, own, peer)
    high = jnp.where(core == 0, peer, own)
    pair = jnp.concatenate([low[:, None], high[:, None]], axis=1)
    turned_cols[...] = pair.reshape(width, wide).T
    @pl.loop(0, blocks)
    def _(step):
        fetch(step).wait()
        count_flat = held.at[step].reshape(BLOCK * tiles, TILE)
        row_block = turned_ref[pl.ds(pl.multiple_of(step * BLOCK, BLOCK), BLOCK), :]
        for chunk in range(width // 256):
            cols = turned_cols[:, chunk * 256 : (chunk + 1) * 256]
            gap_base = jnp.dot(row_block, cols, preferred_element_type=jnp.float32)
            parts = []
            for side in range(2):
                tile = chunk * 2 + side
                cnt = count_flat[pl.ds(tile, BLOCK, stride=tiles), :]
                at_least = jnp.maximum(cnt.astype(jnp.float32), 1.0)
                gap = gap_base[:, side * TILE : (side + 1) * TILE] - jnp.log(at_least)
                slope = jnp.where(
                    cnt > 0,
                    (0.1 + 0.25 * (at_least * lax.rsqrt(at_least))) * gap,
                    1.0 / (1.0 + jnp.exp(-gap)),
                )
                pieces = []
                for sub in range(BLOCK // TILE):
                    mark = occ_ref[step * (BLOCK // TILE) + sub, which * tiles + tile]
                    pieces.append(slope[sub * TILE : (sub + 1) * TILE] * mark.astype(jnp.float32))
                parts.append(jnp.concatenate(pieces, axis=0).astype(jnp.bfloat16))
            residual_ref[
                pl.ds(pl.multiple_of(step * BLOCK, BLOCK), BLOCK), chunk * 256 : (chunk + 1) * 256
            ] = jnp.concatenate(parts, axis=1)

    row_total = lax.dot_general(
        turned_cols[:depth_rows, :], residual_ref[...], (((1,), (1,)), ((), ())),
        preferred_element_type=jnp.float32,
    )
    if not first:
        row_total = row_total + row_in[...]
    row_out[...] = row_total.astype(row_out.dtype)
    col_sum = jnp.dot(
        wide_ref[:depth_rows, :], residual_ref[...], preferred_element_type=jnp.float32
    )
    filled = jnp.concatenate([col_sum, jnp.zeros((wide - depth_rows, width), jnp.float32)], axis=0)
    words_first = filled.T.reshape(chips, 2, 2, 8, wide)
    lane = lax.broadcasted_iota(jnp.int32, (8, TILE), 1)
    for chip in range(chips):
        packed = []
        for side in range(2):
            block = words_first[chip, side]
            last = jnp.where(
                lane < 64, block[0, :, 256:], pltpu.roll(block[1, :, 256:], 64, 1)
            )
            packed.append(
                jnp.concatenate(
                    [block[0, :, :128], block[1, :, :128], block[0, :, 128:256],
                     block[1, :, 128:256], last], axis=0)
            )
        keep_ref[chip] = jnp.where(core == 0, packed[0], packed[1])
        send_ref[chip] = jnp.where(core == 0, packed[1], packed[0])


def run_half(first, occ, counted, wide_rows, turned_rows, own, peer, row_in):
    rows = turned_rows.shape[0]
    chips, wide = own.shape[0], wide_rows.shape[0]
    width = chips * 32
    blocks, tiles = rows // BLOCK, width // TILE
    smem = pl.BlockSpec(memory_space=pltpu.SMEM)
    vmem = pl.BlockSpec(memory_space=pltpu.VMEM)
    operands = [occ, counted, wide_rows, turned_rows, own, peer]
    chunk = jax.ShapeDtypeStruct((chips, PACK, TILE), jnp.float32)
    row_type = jnp.float32 if first else jnp.bfloat16
    out_shape = [jax.ShapeDtypeStruct((304, rows), row_type), chunk, chunk]
    scratch = [pltpu.VMEM((wide, width), jnp.bfloat16), pltpu.VMEM((rows, width), jnp.bfloat16)]
    held = (blocks, BLOCK, tiles, TILE)
    scratch += [pltpu.VMEM(held, jnp.int32), pltpu.SemaphoreType.DMA((blocks,))]
    if not first:
        operands.append(row_in)
    return pl.pallas_call(
        functools.partial(half_step, first),
        in_specs=[smem, pl.BlockSpec(memory_space=pl.ANY)] + [vmem] * (len(operands) - 2),
        out_specs=[vmem] * len(out_shape),
        scratch_shapes=scratch,
        out_shape=out_shape,
        compiler_params=pltpu.CompilerParams(vmem_limit_bytes=HALF_LIMIT),
        cost_estimate=pl.CostEstimate(
            flops=6 * rows * width * 300, bytes_accessed=8 * rows * width // 2,
            transcendentals=rows * width,
        ),
    )(*operands)


def join(keep_a, got_a, keep_b, got_b, out_ref):
    chips = keep_a.shape[0]
    which = lax.axis_index("xl")
    for at, keep, got in ((which, keep_a, got_a), (1 - which, keep_b, got_b)):
        for chip in range(chips):
            out_ref[at * chips + chip] = (keep[chip] + got[chip]).astype(jnp.bfloat16)


def finish(row_scale, col_scale, mine_ref, theirs_ref, got_ref, rows_ref, cols_ref):
    depth = rows_ref.shape[0]
    both = mine_ref[...].astype(jnp.float32) + theirs_ref[...].astype(jnp.float32)
    rows_ref[...] = both[:depth] * row_scale
    total = got_ref[...].astype(jnp.float32).sum(axis=0) * col_scale
    last = total[32:40]
    turned = pltpu.roll(last, 64, 1)
    cols_ref[0:8, :] = jnp.concatenate([total[0:8], total[16:24], last], axis=1)[:, :depth]
    cols_ref[8:16, :] = jnp.concatenate([total[8:16], total[24:32], turned], axis=1)[:, :depth]


def body(row_embed, col_embed, counts, occupancy, row_marg, col_marg, log_total):


    depth, rows = row_embed.shape
    words = col_embed.shape[2]
    params = pltpu.CompilerParams(vmem_limit_bytes=VMEM_LIMIT)
    smem = pl.BlockSpec(memory_space=pltpu.SMEM)
    vmem = pl.BlockSpec(memory_space=pltpu.VMEM)

    fan_out = pl.pallas_call(
        prep_cols,
        out_shape=jax.ShapeDtypeStruct((32, PACK, TILE), jnp.bfloat16),
        compiler_params=params,
    )(col_embed[:, 0, :].T, col_marg)
    quarter = lax.all_to_all(fan_out, ("y", "z"), 0, 0, tiled=True)
    wide_rows, turned_rows = pl.pallas_call(
        prep_rows,
        in_specs=[vmem, vmem, smem],
        out_shape=[
            jax.ShapeDtypeStruct((WIDE, rows), jnp.bfloat16),
            jax.ShapeDtypeStruct((rows, WIDE), jnp.bfloat16),
        ],
        compiler_params=params,
        cost_estimate=pl.CostEstimate(flops=rows * WIDE, bytes_accessed=40 * rows * WIDE, transcendentals=0),
    )(row_embed, row_marg[None, :], log_total)
    quarter, wide_rows, turned_rows = lax.optimization_barrier(
        (quarter, wide_rows, turned_rows)
    )
    count_view = counts.reshape(rows, 16, TILE)
    occ = occupancy[:, 0, :]

    peer = lax.ppermute(quarter, "core", SWAP)
    far = lax.ppermute(quarter, "xl", SWAP)
    row_part, keep_a, send_a = run_half(
        True, occ, count_view, wide_rows, turned_rows, quarter, peer, None
    )
    far, row_part = lax.optimization_barrier((far, row_part))
    far_peer = lax.ppermute(far, "core", SWAP)
    got_a = lax.ppermute(send_a, "core", SWAP)
    mine, keep_b, send_b = run_half(
        False, occ, count_view, wide_rows, turned_rows, far, far_peer, row_part
    )
    got_b = lax.ppermute(send_b, "core", SWAP)
    theirs = lax.ppermute(mine, "xh", SWAP)

    outgoing = pl.pallas_call(
        join,
        in_specs=[vmem] * 4,
        out_shape=jax.ShapeDtypeStruct((64, PACK, TILE), jnp.bfloat16),
        compiler_params=params,
    )(keep_a, got_a, keep_b, got_b)
    arrived = lax.all_to_all(outgoing, ("xl", "y", "z"), 0, 0, tiled=True)
    grad_rows, grad_cols = pl.pallas_call(
        functools.partial(finish, 1.0 / math.sqrt(words * 256), 1.0 / math.sqrt(rows * 128)),
        in_specs=[vmem, vmem, vmem],
        out_specs=[vmem, vmem],
        out_shape=[
            jax.ShapeDtypeStruct((depth, rows), jnp.float32),
            jax.ShapeDtypeStruct((words, depth), jnp.float32),
        ],
        compiler_params=params,
    )(mine, theirs, arrived)
    return (grad_rows, grad_cols.T[:, None, :])


def solution(mesh):
    fine = Mesh(mesh.devices.reshape(SPLIT), AXES)
    placed = (
        P(None, ROW),
        P(None, "xh", ROW),
        P(ROW, "xh", None),
        P(ROW, "xh", None),
        P(ROW),
        P("xh", ROW),
        P(),
    )
    return jax.shard_map(
        body,
        mesh=fine,
        in_specs=placed,
        out_specs=(P(None, ROW), P(None, "xh", ROW)),
        check_vma=False,
    )
```

```python
import functools
import math

import jax
import jax.numpy as jnp
from jax import lax
from jax.experimental import pallas as pl
from jax.experimental.pallas import tpu as pltpu
from jax.sharding import Mesh, PartitionSpec as P

SPLIT = (2, 4, 8, 2, 2)
AXES = ("xl", "y", "z", "core", "xh")
ROW = ("xl", "y", "z", "core")
TILE = 128
WIDE = 384
BLOCK = 256
PACK = 40
FINISH_FLOPS = 100_000_000_000
VMEM_LIMIT = 24 * 1024 * 1024
HALF_LIMIT = 48 * 1024 * 1024
SWAP = [(0, 1), (1, 0)]


def three_parts(values):
    high = values.astype(jnp.bfloat16).astype(jnp.float32)
    rest = values - high
    middle = rest.astype(jnp.bfloat16).astype(jnp.float32)
    return high, middle, rest - middle


def prep_cols(embed_ref, marg_ref, out_ref):
    copies = out_ref.shape[0]
    words, depth = embed_ref.shape
    log_col = jnp.log(marg_ref[...].astype(jnp.float32))
    square = (words, words)
    same = lax.broadcasted_iota(jnp.int32, square, 0) == lax.broadcasted_iota(jnp.int32, square, 1)
    spread = jnp.where(same, jnp.broadcast_to(log_col, square), 0.0).sum(axis=1, keepdims=True)
    high, middle, low = three_parts(spread)
    embed = embed_ref[...].astype(jnp.float32)
    lane = lax.broadcasted_iota(jnp.int32, (words, WIDE - 256), 1) + 256
    tail = jnp.where(lane == depth, high, 0.0)
    tail = jnp.where(lane == depth + 1, middle, tail)
    tail = jnp.where(lane == depth + 2, low, tail)
    tail = jnp.where((lane >= depth + 3) & (lane < depth + 6), 1.0, tail)
    padded = jnp.concatenate([embed, jnp.zeros((words, WIDE - depth), jnp.float32)], axis=1)
    tail = tail + padded[:, 256:]
    half_lane = lax.broadcasted_iota(jnp.int32, (8, TILE), 1)
    last = jnp.where(half_lane < 64, tail[:8], pltpu.roll(tail[8:], 64, 1))
    block = jnp.concatenate([padded[:, :128], padded[:, 128:256], last], axis=0).astype(jnp.bfloat16)
    for copy in range(copies):
        out_ref[copy] = block


def unpack_words(packed):
    blocks = packed.astype(jnp.float32)
    last = blocks[:, 32:40, :]
    lane = lax.broadcasted_iota(jnp.int32, last.shape, 2)
    front = jnp.where(lane < 64, last, 0.0)
    back = jnp.where(lane < 64, pltpu.roll(last, 64, 2), 0.0)
    tail = jnp.concatenate([front, back], axis=1)
    whole = jnp.concatenate([blocks[:, :16, :], blocks[:, 16:32, :], tail], axis=2)
    return whole.astype(jnp.bfloat16)


def prep_rows(embed_ref, marg_ref, total_ref, wide_ref, turned_ref):
    depth, rows = embed_ref.shape
    wide = wide_ref.shape[0]
    log_row = jnp.log(marg_ref[...].astype(jnp.float32)) - total_ref[0]
    high, middle, low = three_parts(log_row)
    start = depth - depth % 8
    line = lax.broadcasted_iota(jnp.int32, (wide - start, rows), 0) + start
    tail = jnp.where((line >= depth) & (line < depth + 3), 1.0, 0.0)
    tail = jnp.where(line == depth + 3, high, tail)
    tail = jnp.where(line == depth + 4, middle, tail)
    tail = jnp.where(line == depth + 5, low, tail)
    embed = embed_ref[...].astype(jnp.float32)
    padded = jnp.concatenate([embed, jnp.zeros((wide - depth, rows), jnp.float32)], axis=0)
    whole = jnp.concatenate([padded[:start], padded[start:] + tail], axis=0)
    wide_ref[...] = whole.astype(jnp.bfloat16)
    turned_ref[...] = whole.T.astype(jnp.bfloat16)


def half_step(first, occ_ref, count_ref, wide_ref, turned_ref, own_ref, peer_ref, *rest):
    if first:
        row_out, keep_ref, send_ref, turned_cols, residual_ref, held, arrived = rest
    else:
        row_in, row_out, keep_ref, send_ref, turned_cols, residual_ref, held, arrived = rest
    xl, core = lax.axis_index("xl"), lax.axis_index("core")
    which = xl if first else 1 - xl
    chips = own_ref.shape[0]
    wide = wide_ref.shape[0]
    depth_rows = 304
    rows, width = residual_ref.shape
    tiles = width // TILE
    blocks = rows // BLOCK

    def fetch(step):
        return pltpu.make_async_copy(
            count_ref.at[
                pl.ds(step * BLOCK, BLOCK), pl.ds(pl.multiple_of(which * tiles, tiles), tiles), :
            ],
            held.at[step],
            arrived.at[step],
        )

    for step in range(blocks):
        fetch(step).start()

    own, peer = unpack_words(own_ref[...]), unpack_words(peer_ref[...])
    low = jnp.where(core == 0, own, peer)
    high = jnp.where(core == 0, peer, own)
    pair = jnp.concatenate([low[:, None], high[:, None]], axis=1)
    turned_cols[...] = pair.reshape(width, wide).T
    @pl.loop(0, blocks, unroll=True)
    def _(step):
        fetch(step).wait()
        count_flat = held.at[step].reshape(BLOCK * tiles, TILE)
        row_block = turned_ref[pl.ds(pl.multiple_of(step * BLOCK, BLOCK), BLOCK), :]
        for chunk in range(width // 256):
            cols = turned_cols[:, chunk * 256 : (chunk + 1) * 256]
            gap_base = jnp.dot(row_block, cols, preferred_element_type=jnp.float32)
            parts = []
            for side in range(2):
                tile = chunk * 2 + side
                cnt = count_flat[pl.ds(tile, BLOCK, stride=tiles), :]
                at_least = jnp.maximum(cnt.astype(jnp.float32), 1.0)
                gap = gap_base[:, side * TILE : (side + 1) * TILE] - jnp.log(at_least)
                slope = jnp.where(
                    cnt > 0,
                    (0.1 + 0.25 * (at_least * lax.rsqrt(at_least))) * gap,
                    1.0 / (1.0 + jnp.exp(-gap)),
                )
                pieces = []
                for sub in range(BLOCK // TILE):
                    mark = occ_ref[step * (BLOCK // TILE) + sub, which * tiles + tile]
                    pieces.append(slope[sub * TILE : (sub + 1) * TILE] * mark.astype(jnp.float32))
                parts.append(jnp.concatenate(pieces, axis=0).astype(jnp.bfloat16))
            residual_ref[
                pl.ds(pl.multiple_of(step * BLOCK, BLOCK), BLOCK), chunk * 256 : (chunk + 1) * 256
            ] = jnp.concatenate(parts, axis=1)

    row_total = lax.dot_general(
        turned_cols[:depth_rows, :], residual_ref[...], (((1,), (1,)), ((), ())),
        preferred_element_type=jnp.float32,
    )
    if not first:
        row_total = row_total + row_in[...]
    row_out[...] = row_total.astype(row_out.dtype)
    col_sum = jnp.dot(
        wide_ref[:depth_rows, :], residual_ref[...], preferred_element_type=jnp.float32
    )
    filled = jnp.concatenate([col_sum, jnp.zeros((wide - depth_rows, width), jnp.float32)], axis=0)
    words_first = filled.T.reshape(chips, 2, 2, 8, wide)
    lane = lax.broadcasted_iota(jnp.int32, (8, TILE), 1)
    for chip in range(chips):
        packed = []
        for side in range(2):
            block = words_first[chip, side]
            last = jnp.where(
                lane < 64, block[0, :, 256:], pltpu.roll(block[1, :, 256:], 64, 1)
            )
            packed.append(
                jnp.concatenate(
                    [block[0, :, :128], block[1, :, :128], block[0, :, 128:256],
                     block[1, :, 128:256], last], axis=0)
            )
        keep_ref[chip] = jnp.where(core == 0, packed[0], packed[1])
        send_ref[chip] = jnp.where(core == 0, packed[1], packed[0])


def run_half(first, occ, counted, wide_rows, turned_rows, own, peer, row_in):
    rows = turned_rows.shape[0]
    chips, wide = own.shape[0], wide_rows.shape[0]
    width = chips * 32
    blocks, tiles = rows // BLOCK, width // TILE
    smem = pl.BlockSpec(memory_space=pltpu.SMEM)
    vmem = pl.BlockSpec(memory_space=pltpu.VMEM)
    operands = [occ, counted, wide_rows, turned_rows, own, peer]
    chunk = jax.ShapeDtypeStruct((chips, PACK, TILE), jnp.float32)
    row_type = jnp.float32 if first else jnp.bfloat16
    out_shape = [jax.ShapeDtypeStruct((304, rows), row_type), chunk, chunk]
    scratch = [pltpu.VMEM((wide, width), jnp.bfloat16), pltpu.VMEM((rows, width), jnp.bfloat16)]
    held = (blocks, BLOCK, tiles, TILE)
    scratch += [pltpu.VMEM(held, jnp.int32), pltpu.SemaphoreType.DMA((blocks,))]
    if not first:
        operands.append(row_in)
    return pl.pallas_call(
        functools.partial(half_step, first),
        in_specs=[smem, pl.BlockSpec(memory_space=pl.ANY)] + [vmem] * (len(operands) - 2),
        out_specs=[vmem] * len(out_shape),
        scratch_shapes=scratch,
        out_shape=out_shape,
        compiler_params=pltpu.CompilerParams(vmem_limit_bytes=HALF_LIMIT),
        cost_estimate=pl.CostEstimate(
            flops=6 * rows * width * 300, bytes_accessed=8 * rows * width // 2,
            transcendentals=rows * width,
        ),
    )(*operands)


def join(keep_a, got_a, keep_b, got_b, out_ref):
    chips = keep_a.shape[0]
    which = lax.axis_index("xl")
    for at, keep, got in ((which, keep_a, got_a), (1 - which, keep_b, got_b)):
        for chip in range(chips):
            out_ref[at * chips + chip] = (keep[chip] + got[chip]).astype(jnp.bfloat16)


def finish_rows(scale, mine_ref, theirs_ref, out_ref):
    both = mine_ref[...].astype(jnp.float32) + theirs_ref[...].astype(jnp.float32)
    out_ref[...] = both[: out_ref.shape[0]] * scale


def finish_cols(scale, got_ref, out_ref):
    depth = out_ref.shape[1]
    total = got_ref[...].astype(jnp.float32).sum(axis=0) * scale
    last = total[32:40]
    turned = pltpu.roll(last, 64, 1)
    out_ref[0:8, :] = jnp.concatenate([total[0:8], total[16:24], last], axis=1)[:, :depth]
    out_ref[8:16, :] = jnp.concatenate([total[8:16], total[24:32], turned], axis=1)[:, :depth]


def body(row_embed, col_embed, counts, occupancy, row_marg, col_marg, log_total):


    depth, rows = row_embed.shape
    words = col_embed.shape[2]
    params = pltpu.CompilerParams(vmem_limit_bytes=VMEM_LIMIT)
    smem = pl.BlockSpec(memory_space=pltpu.SMEM)
    vmem = pl.BlockSpec(memory_space=pltpu.VMEM)

    fan_out = pl.pallas_call(
        prep_cols,
        out_shape=jax.ShapeDtypeStruct((32, PACK, TILE), jnp.bfloat16),
        compiler_params=params,
    )(col_embed[:, 0, :].T, col_marg)
    quarter = lax.all_to_all(fan_out, ("y", "z"), 0, 0, tiled=True)
    wide_rows, turned_rows = pl.pallas_call(
        prep_rows,
        in_specs=[vmem, vmem, smem],
        out_shape=[
            jax.ShapeDtypeStruct((WIDE, rows), jnp.bfloat16),
            jax.ShapeDtypeStruct((rows, WIDE), jnp.bfloat16),
        ],
        compiler_params=params,
        cost_estimate=pl.CostEstimate(flops=rows * WIDE, bytes_accessed=40 * rows * WIDE, transcendentals=0),
    )(row_embed, row_marg[None, :], log_total)
    quarter, wide_rows, turned_rows = lax.optimization_barrier(
        (quarter, wide_rows, turned_rows)
    )
    count_view = counts.reshape(rows, 16, TILE)
    occ = occupancy[:, 0, :]

    peer = lax.ppermute(quarter, "core", SWAP)
    far = lax.ppermute(quarter, "xl", SWAP)
    row_part, keep_a, send_a = run_half(
        True, occ, count_view, wide_rows, turned_rows, quarter, peer, None
    )
    far, row_part = lax.optimization_barrier((far, row_part))
    far_peer = lax.ppermute(far, "core", SWAP)
    got_a = lax.ppermute(send_a, "core", SWAP)
    mine, keep_b, send_b = run_half(
        False, occ, count_view, wide_rows, turned_rows, far, far_peer, row_part
    )
    got_b = lax.ppermute(send_b, "core", SWAP)
    theirs = lax.ppermute(mine, "xh", SWAP)

    outgoing = pl.pallas_call(
        join,
        in_specs=[vmem] * 4,
        out_shape=jax.ShapeDtypeStruct((64, PACK, TILE), jnp.bfloat16),
        compiler_params=params,
    )(keep_a, got_a, keep_b, got_b)
    arrived = lax.all_to_all(outgoing, ("xl", "y", "z"), 0, 0, tiled=True)
    grad_rows = pl.pallas_call(
        functools.partial(finish_rows, 1.0 / math.sqrt(words * 256)),
        out_shape=jax.ShapeDtypeStruct((depth, rows), jnp.float32),
        compiler_params=params,
        cost_estimate=pl.CostEstimate(
            flops=FINISH_FLOPS, bytes_accessed=4 * depth * rows * 2, transcendentals=0
        ),
    )(mine, theirs)
    grad_cols = pl.pallas_call(
        functools.partial(finish_cols, 1.0 / math.sqrt(rows * 128)),
        out_shape=jax.ShapeDtypeStruct((words, depth), jnp.float32),
        compiler_params=params,
    )(arrived)
    return (grad_rows, grad_cols.T[:, None, :])


def solution(mesh):
    fine = Mesh(mesh.devices.reshape(SPLIT), AXES)
    placed = (
        P(None, ROW),
        P(None, "xh", ROW),
        P(ROW, "xh", None),
        P(ROW, "xh", None),
        P(ROW),
        P("xh", ROW),
        P(),
    )
    return jax.shard_map(
        body,
        mesh=fine,
        in_specs=placed,
        out_specs=(P(None, ROW), P(None, "xh", ROW)),
        check_vma=False,
    )
```

```python
import functools
import math

import jax
import jax.numpy as jnp
from jax import lax
from jax.experimental import pallas as pl
from jax.experimental.pallas import tpu as pltpu
from jax.sharding import Mesh, PartitionSpec as P

SPLIT = (2, 4, 8, 2, 2)
AXES = ("xl", "y", "z", "core", "xh")
ROW = ("xl", "y", "z", "core")
TILE = 128
WIDE = 384
BLOCK = 256
PACK = 40
FINISH_FLOPS = 100_000_000_000
VMEM_LIMIT = 24 * 1024 * 1024
HALF_LIMIT = 48 * 1024 * 1024
SWAP = [(0, 1), (1, 0)]


def three_parts(values):
    high = values.astype(jnp.bfloat16).astype(jnp.float32)
    rest = values - high
    middle = rest.astype(jnp.bfloat16).astype(jnp.float32)
    return high, middle, rest - middle


def prep_cols(embed_ref, marg_ref, out_ref):
    copies = out_ref.shape[0]
    words, depth = embed_ref.shape
    log_col = jnp.log(marg_ref[...].astype(jnp.float32))
    square = (words, words)
    same = lax.broadcasted_iota(jnp.int32, square, 0) == lax.broadcasted_iota(jnp.int32, square, 1)
    spread = jnp.where(same, jnp.broadcast_to(log_col, square), 0.0).sum(axis=1, keepdims=True)
    high, middle, low = three_parts(spread)
    embed = embed_ref[...].astype(jnp.float32)
    lane = lax.broadcasted_iota(jnp.int32, (words, WIDE - 256), 1) + 256
    tail = jnp.where(lane == depth, high, 0.0)
    tail = jnp.where(lane == depth + 1, middle, tail)
    tail = jnp.where(lane == depth + 2, low, tail)
    tail = jnp.where((lane >= depth + 3) & (lane < depth + 6), 1.0, tail)
    padded = jnp.concatenate([embed, jnp.zeros((words, WIDE - depth), jnp.float32)], axis=1)
    tail = tail + padded[:, 256:]
    half_lane = lax.broadcasted_iota(jnp.int32, (8, TILE), 1)
    last = jnp.where(half_lane < 64, tail[:8], pltpu.roll(tail[8:], 64, 1))
    block = jnp.concatenate([padded[:, :128], padded[:, 128:256], last], axis=0).astype(jnp.bfloat16)
    for copy in range(copies):
        out_ref[copy] = block


def unpack_words(packed):
    blocks = packed.astype(jnp.float32)
    last = blocks[:, 32:40, :]
    lane = lax.broadcasted_iota(jnp.int32, last.shape, 2)
    front = jnp.where(lane < 64, last, 0.0)
    back = jnp.where(lane < 64, pltpu.roll(last, 64, 2), 0.0)
    tail = jnp.concatenate([front, back], axis=1)
    whole = jnp.concatenate([blocks[:, :16, :], blocks[:, 16:32, :], tail], axis=2)
    return whole.astype(jnp.bfloat16)


def prep_rows(embed_ref, marg_ref, total_ref, wide_ref, turned_ref):
    depth, rows = embed_ref.shape
    wide = wide_ref.shape[0]
    log_row = jnp.log(marg_ref[...].astype(jnp.float32)) - total_ref[0]
    high, middle, low = three_parts(log_row)
    start = depth - depth % 8
    line = lax.broadcasted_iota(jnp.int32, (wide - start, rows), 0) + start
    tail = jnp.where((line >= depth) & (line < depth + 3), 1.0, 0.0)
    tail = jnp.where(line == depth + 3, high, tail)
    tail = jnp.where(line == depth + 4, middle, tail)
    tail = jnp.where(line == depth + 5, low, tail)
    embed = embed_ref[...].astype(jnp.float32)
    padded = jnp.concatenate([embed, jnp.zeros((wide - depth, rows), jnp.float32)], axis=0)
    whole = jnp.concatenate([padded[:start], padded[start:] + tail], axis=0)
    wide_ref[...] = whole.astype(jnp.bfloat16)
    turned_ref[...] = whole.T.astype(jnp.bfloat16)


def half_step(first, occ_ref, count_ref, wide_ref, turned_ref, own_ref, peer_ref, *rest):
    if first:
        row_out, keep_ref, send_ref, turned_cols, residual_ref, held, arrived = rest
    else:
        row_in, row_out, keep_ref, send_ref, turned_cols, residual_ref, held, arrived = rest
    xl, core = lax.axis_index("xl"), lax.axis_index("core")
    which = xl if first else 1 - xl
    chips = own_ref.shape[0]
    wide = wide_ref.shape[0]
    depth_rows = 304
    rows, width = residual_ref.shape
    tiles = width // TILE
    blocks = rows // BLOCK

    def fetch(step):
        return pltpu.make_async_copy(
            count_ref.at[
                pl.ds(step * BLOCK, BLOCK), pl.ds(pl.multiple_of(which * tiles, tiles), tiles), :
            ],
            held.at[step],
            arrived.at[step],
        )

    for step in range(blocks):
        fetch(step).start()

    own, peer = unpack_words(own_ref[...]), unpack_words(peer_ref[...])
    low = jnp.where(core == 0, own, peer)
    high = jnp.where(core == 0, peer, own)
    pair = jnp.concatenate([low[:, None], high[:, None]], axis=1)
    turned_cols[...] = pair.reshape(width, wide).T
    @pl.loop(0, blocks, unroll=True)
    def _(step):
        fetch(step).wait()
        count_flat = held.at[step].reshape(BLOCK * tiles, TILE)
        row_block = turned_ref[pl.ds(pl.multiple_of(step * BLOCK, BLOCK), BLOCK), :]
        for chunk in range(width // 256):
            cols = turned_cols[:, chunk * 256 : (chunk + 1) * 256]
            gap_base = jnp.dot(row_block, cols, preferred_element_type=jnp.float32)
            parts = []
            for side in range(2):
                tile = chunk * 2 + side
                cnt = count_flat[pl.ds(tile, BLOCK, stride=tiles), :]
                at_least = jnp.maximum(cnt.astype(jnp.float32), 1.0)
                gap = gap_base[:, side * TILE : (side + 1) * TILE] - jnp.log(at_least)
                slope = jnp.where(
                    cnt > 0,
                    (0.1 + 0.25 * (at_least * lax.rsqrt(at_least))) * gap,
                    1.0 / (1.0 + jnp.exp(-gap)),
                )
                pieces = []
                for sub in range(BLOCK // TILE):
                    mark = occ_ref[step * (BLOCK // TILE) + sub, which * tiles + tile]
                    pieces.append(slope[sub * TILE : (sub + 1) * TILE] * mark.astype(jnp.float32))
                parts.append(jnp.concatenate(pieces, axis=0).astype(jnp.bfloat16))
            residual_ref[
                pl.ds(pl.multiple_of(step * BLOCK, BLOCK), BLOCK), chunk * 256 : (chunk + 1) * 256
            ] = jnp.concatenate(parts, axis=1)

    row_total = lax.dot_general(
        turned_cols[:depth_rows, :], residual_ref[...], (((1,), (1,)), ((), ())),
        preferred_element_type=jnp.float32,
    )
    if not first:
        row_total = row_total + row_in[...]
    row_out[...] = row_total.astype(row_out.dtype)
    col_sum = jnp.dot(
        wide_ref[:depth_rows, :], residual_ref[...], preferred_element_type=jnp.float32
    )
    filled = jnp.concatenate([col_sum, jnp.zeros((wide - depth_rows, width), jnp.float32)], axis=0)
    words_first = filled.T.reshape(chips, 2, 2, 8, wide)
    lane = lax.broadcasted_iota(jnp.int32, (8, TILE), 1)
    for chip in range(chips):
        packed = []
        for side in range(2):
            block = words_first[chip, side]
            last = jnp.where(
                lane < 64, block[0, :, 256:], pltpu.roll(block[1, :, 256:], 64, 1)
            )
            packed.append(
                jnp.concatenate(
                    [block[0, :, :128], block[1, :, :128], block[0, :, 128:256],
                     block[1, :, 128:256], last], axis=0)
            )
        keep_ref[chip] = jnp.where(core == 0, packed[0], packed[1])
        send_ref[chip] = jnp.where(core == 0, packed[1], packed[0])


def run_half(first, occ, counted, wide_rows, turned_rows, own, peer, row_in):
    rows = turned_rows.shape[0]
    chips, wide = own.shape[0], wide_rows.shape[0]
    width = chips * 32
    blocks, tiles = rows // BLOCK, width // TILE
    smem = pl.BlockSpec(memory_space=pltpu.SMEM)
    vmem = pl.BlockSpec(memory_space=pltpu.VMEM)
    operands = [occ, counted, wide_rows, turned_rows, own, peer]
    chunk = jax.ShapeDtypeStruct((chips, PACK, TILE), jnp.float32)
    row_type = jnp.float32 if first else jnp.bfloat16
    out_shape = [jax.ShapeDtypeStruct((304, rows), row_type), chunk, chunk]
    scratch = [pltpu.VMEM((wide, width), jnp.bfloat16), pltpu.VMEM((rows, width), jnp.bfloat16)]
    held = (blocks, BLOCK, tiles, TILE)
    scratch += [pltpu.VMEM(held, jnp.int32), pltpu.SemaphoreType.DMA((blocks,))]
    if not first:
        operands.append(row_in)
    return pl.pallas_call(
        functools.partial(half_step, first),
        in_specs=[smem, pl.BlockSpec(memory_space=pl.ANY)] + [vmem] * (len(operands) - 2),
        out_specs=[vmem] * len(out_shape),
        scratch_shapes=scratch,
        out_shape=out_shape,
        compiler_params=pltpu.CompilerParams(vmem_limit_bytes=HALF_LIMIT),
        cost_estimate=pl.CostEstimate(
            flops=6 * rows * width * 300, bytes_accessed=8 * rows * width // 2,
            transcendentals=rows * width,
        ),
    )(*operands)


def join_near(keep, got, out_ref):
    chips = keep.shape[0]
    for chip in range(chips):
        out_ref[chip] = (keep[chip] + got[chip]).astype(jnp.bfloat16)


def join_far(keep, got, near_ref, out_ref):
    chips = keep.shape[0]
    for chip in range(chips):
        out_ref[lax.axis_index("xl") * chips + chip] = near_ref[chip]
        out_ref[(1 - lax.axis_index("xl")) * chips + chip] = (keep[chip] + got[chip]).astype(
            jnp.bfloat16
        )


def finish_rows(scale, mine_ref, theirs_ref, out_ref):
    both = mine_ref[...].astype(jnp.float32) + theirs_ref[...].astype(jnp.float32)
    out_ref[...] = both[: out_ref.shape[0]] * scale


def finish_cols(scale, got_ref, out_ref):
    depth = out_ref.shape[1]
    total = got_ref[...].astype(jnp.float32).sum(axis=0) * scale
    last = total[32:40]
    turned = pltpu.roll(last, 64, 1)
    out_ref[0:8, :] = jnp.concatenate([total[0:8], total[16:24], last], axis=1)[:, :depth]
    out_ref[8:16, :] = jnp.concatenate([total[8:16], total[24:32], turned], axis=1)[:, :depth]


def body(row_embed, col_embed, counts, occupancy, row_marg, col_marg, log_total):


    depth, rows = row_embed.shape
    words = col_embed.shape[2]
    params = pltpu.CompilerParams(vmem_limit_bytes=VMEM_LIMIT)
    smem = pl.BlockSpec(memory_space=pltpu.SMEM)
    vmem = pl.BlockSpec(memory_space=pltpu.VMEM)

    fan_out = pl.pallas_call(
        prep_cols,
        out_shape=jax.ShapeDtypeStruct((32, PACK, TILE), jnp.bfloat16),
        compiler_params=params,
    )(col_embed[:, 0, :].T, col_marg)
    quarter = lax.all_to_all(fan_out, ("y", "z"), 0, 0, tiled=True)
    wide_rows, turned_rows = pl.pallas_call(
        prep_rows,
        in_specs=[vmem, vmem, smem],
        out_shape=[
            jax.ShapeDtypeStruct((WIDE, rows), jnp.bfloat16),
            jax.ShapeDtypeStruct((rows, WIDE), jnp.bfloat16),
        ],
        compiler_params=params,
        cost_estimate=pl.CostEstimate(flops=rows * WIDE, bytes_accessed=40 * rows * WIDE, transcendentals=0),
    )(row_embed, row_marg[None, :], log_total)
    quarter, wide_rows, turned_rows = lax.optimization_barrier(
        (quarter, wide_rows, turned_rows)
    )
    count_view = counts.reshape(rows, 16, TILE)
    occ = occupancy[:, 0, :]

    peer = lax.ppermute(quarter, "core", SWAP)
    far = lax.ppermute(quarter, "xl", SWAP)
    row_part, keep_a, send_a = run_half(
        True, occ, count_view, wide_rows, turned_rows, quarter, peer, None
    )
    far, row_part = lax.optimization_barrier((far, row_part))
    far_peer = lax.ppermute(far, "core", SWAP)
    got_a = lax.ppermute(send_a, "core", SWAP)
    mine, keep_b, send_b = run_half(
        False, occ, count_view, wide_rows, turned_rows, far, far_peer, row_part
    )
    got_b = lax.ppermute(send_b, "core", SWAP)
    theirs = lax.ppermute(mine, "xh", SWAP)

    whole = jax.ShapeDtypeStruct((64, PACK, TILE), jnp.bfloat16)
    near = jax.ShapeDtypeStruct((32, PACK, TILE), jnp.bfloat16)
    outgoing = pl.pallas_call(
        join_near, in_specs=[vmem] * 2, out_specs=vmem, out_shape=near, compiler_params=params
    )(keep_a, got_a)
    outgoing = pl.pallas_call(
        join_far,
        in_specs=[vmem] * 3,
        out_specs=vmem,
        out_shape=whole,
        compiler_params=params,
    )(keep_b, got_b, outgoing)
    arrived = lax.all_to_all(outgoing, ("xl", "y", "z"), 0, 0, tiled=True)
    grad_rows = pl.pallas_call(
        functools.partial(finish_rows, 1.0 / math.sqrt(words * 256)),
        out_shape=jax.ShapeDtypeStruct((depth, rows), jnp.float32),
        compiler_params=params,
        cost_estimate=pl.CostEstimate(
            flops=FINISH_FLOPS, bytes_accessed=4 * depth * rows * 2, transcendentals=0
        ),
    )(mine, theirs)
    grad_cols = pl.pallas_call(
        functools.partial(finish_cols, 1.0 / math.sqrt(rows * 128)),
        out_shape=jax.ShapeDtypeStruct((words, depth), jnp.float32),
        compiler_params=params,
    )(arrived)
    return (grad_rows, grad_cols.T[:, None, :])


def solution(mesh):
    fine = Mesh(mesh.devices.reshape(SPLIT), AXES)
    placed = (
        P(None, ROW),
        P(None, "xh", ROW),
        P(ROW, "xh", None),
        P(ROW, "xh", None),
        P(ROW),
        P("xh", ROW),
        P(),
    )
    return jax.shard_map(
        body,
        mesh=fine,
        in_specs=placed,
        out_specs=(P(None, ROW), P(None, "xh", ROW)),
        check_vma=False,
    )
```
